1024 devices in a mesh: section: 16 (over y, x_lo), replica: 64 (over z, x_hi, core).
Axes of the slice: x: 4 (x_hi: 2, x_lo: 2; x = x_hi * 2 + x_lo), y: 8, z: 16, core: 2. Of those that a mesh axis runs over, the one named last changes fastest.
Arguments:
- hidden: bfloat16 [16, 16384, 64], P('section', 'replica'), may hold values from -16 to 16
- out_grad: bfloat16 [16, 16384, 6144], P('section', 'replica'), may hold values from -6 to 6
- weights_old: bfloat16 [1024, 6144], P('section'), may hold values from -6 to 6
- master: float32 [1024, 6144], P(('section', 'replica')), may hold values from -6 to 6
- first_moment: float32 [1024, 6144], P(('section', 'replica')), may hold values from -4 to 4
- second_moment: float32 [1024, 6144], P(('section', 'replica')), may hold values from 0.01 to 1
- owner_order: int32 [64], replicated, may hold values from 0 to 63, each once
- step_count: int32 [1], replicated, may hold values from 1 to 8
Outputs:
- new_master: float32 [1024, 6144], P(('section', 'replica'))
- new_first: float32 [1024, 6144], P(('section', 'replica'))
- new_second: float32 [1024, 6144], P(('section', 'replica'))
- checkpoint: float32 [3, 1024, 6144], P(None, ('section', 'replica'))
- weights_new: bfloat16 [1024, 6144], P('section')
- hidden_grad: bfloat16 [16, 16384, 64], P('section', 'replica')
The draws below stay inside these ranges and needn't reach their ends.
Inputs may be any that keep to these rules, and one draw needn't show every extreme that they name: Replica r owns block owner_order[r] of its section's bucket.
All inputs are finite; a program needn't handle non-finite values.
Results may differ from the reference program's by a relative error of at most 0.005.
Values may be sent and summed in bfloat16 or wider, within the bound.
A program may use at most 32 MiB of HBM per device.

```python
import math
import jax
import jax.numpy as jnp
from jax import lax

D = 6144
SLAB_ROWS = 64
TOK_DEV = 256
TOKENS = 16384
SECTIONS = 16
N_SECTION = 16
N_REPLICA = 64


def strengthened(drawn, key, source, target, blocks, factor):
    def block_of(position):
        return (jnp.arange(drawn.shape[position]) // (drawn.shape[position] // blocks)).reshape((-1,) + (1,) * (drawn.ndim - 1 - position))

    near = jax.random.permutation(key, blocks)[block_of(target)]
    other_side = (block_of(target) + blocks // 2) % blocks
    return jnp.where((block_of(source) == near) | (block_of(source) == other_side), factor * drawn, drawn)


def shard_levels(own_key, shape, cuts, least, top_value):
    loudness = 1.0
    for axis_at, blocks in cuts:
        draws = jax.random.uniform(jax.random.fold_in(jax.random.fold_in(own_key, 6), axis_at), (blocks,), jnp.float32, least / len(cuts), top_value / len(cuts))
        loudness = loudness * jnp.repeat(jnp.exp(draws), shape[axis_at] // blocks).reshape((-1,) + (1,) * (len(shape) - 1 - axis_at))
    return loudness


def bell_draw(own_key, dims, width, bound, shards=(), kind=jnp.bfloat16):
    drawn = width * jax.random.normal(own_key, dims, jnp.float32)
    if shards:
        drawn = drawn * shard_levels(own_key, dims, shards, -0.22, 0.18)
    return jnp.clip(drawn, -bound, bound).astype(kind)


def noise_with(stream_key, shape, deviation, limit, shards, heavy, kind=jnp.bfloat16):
    array = deviation * jax.random.normal(stream_key, shape, jnp.float32)
    if shards:
        array = array * shard_levels(stream_key, shape, shards, -0.22, 0.18)
    return jnp.clip(strengthened(array, jax.random.fold_in(stream_key, 3), *heavy), -limit, limit).astype(kind)


def setup_inputs(seed: int = 0) -> dict:
    arg_keys = jax.random.split(jax.random.key(seed), 9)
    hidden = noise_with(arg_keys[0], (SECTIONS, TOKENS, SLAB_ROWS), 1.0, 16.0, ((0, 16), (1, 64)), (1, 2, 64, 4.0))
    out_grad = bell_draw(arg_keys[1], (SECTIONS, TOKENS, D), 1.0, 6.0, ((0, 16), (1, 64)))
    weights_old = bell_draw(arg_keys[2], (SECTIONS * SLAB_ROWS, D), 1.0, 6.0, ((0, 16),))
    master = bell_draw(arg_keys[3], (SECTIONS * SLAB_ROWS, D), 1.0, 6.0, ((0, 1024),), jnp.float32)
    first_moment = bell_draw(arg_keys[4], (SECTIONS * SLAB_ROWS, D), 0.3, 4.0, ((0, 1024),), jnp.float32)
    second_moment = jnp.clip(jnp.exp(math.log(1.0) - 4.6051702 * jax.random.uniform(arg_keys[5], (SECTIONS * SLAB_ROWS, D), jnp.float32) ** shard_levels(arg_keys[5], (SECTIONS * SLAB_ROWS, D), ((0, 1024),), -0.2, 0.2)), 0.01, 1.0)
    owner_order = jax.random.permutation(arg_keys[6], N_REPLICA).astype(jnp.int32)
    step_count = jax.random.randint(arg_keys[7], (1,), 1, 9).astype(jnp.int32)
    return dict(hidden=hidden, out_grad=out_grad, weights_old=weights_old, master=master, first_moment=first_moment, second_moment=second_moment, owner_order=owner_order, step_count=step_count)


def adam_update(grads, master, first, second, steps):
    first_new = 0.9 * first + 0.1 * grads
    second_new = 0.95 * second + 0.05 * grads * grads
    fix_one = 1.0 - jnp.power(0.9, steps)
    fix_two = 1.0 - jnp.power(0.95, steps)
    update = first_new / fix_one / (jnp.sqrt(second_new / fix_two) + 1e-08)
    master_new = master - 0.05 * (update + 0.1 * master)
    return (master_new, first_new, second_new)

def reference(hidden, out_grad, weights_old, master, first_moment, second_moment, owner_order, step_count):
    factor = D ** (-0.5)
    block = SLAB_ROWS // N_REPLICA

    def per_section(operands):
        acts, grads_out, slab = operands
        slab_grad = lax.dot_general(acts, grads_out, (((0,), (0,)), ((), ())), preferred_element_type=jnp.float32) / TOK_DEV
        back = lax.dot_general(grads_out, slab, (((1,), (1,)), ((), ())), preferred_element_type=jnp.float32)
        return (slab_grad, (back * factor).astype(jnp.bfloat16))
    slab_grads, hidden_grad = lax.map(per_section, (hidden, out_grad, weights_old.reshape(N_SECTION, SLAB_ROWS, D)))
    owned = jnp.take(slab_grads.reshape(N_SECTION, N_REPLICA, block, D), owner_order, axis=1).reshape(N_SECTION * SLAB_ROWS, D)
    steps = step_count[0].astype(jnp.float32)
    new_master, new_first, new_second = adam_update(owned, master, first_moment, second_moment, steps)
    stacked = jnp.stack([new_master, new_first, new_second]).reshape(3, N_SECTION, N_REPLICA, block, D)
    checkpoint = jnp.roll(stacked, 1, axis=2).reshape(3, N_SECTION * SLAB_ROWS, D)
    inverse = jnp.zeros((N_REPLICA,), jnp.int32).at[owner_order].set(jnp.arange(N_REPLICA, dtype=jnp.int32))
    rounded = new_master.astype(jnp.bfloat16).reshape(N_SECTION, N_REPLICA, block, D)
    weights_new = jnp.take(rounded, inverse, axis=1).reshape(N_SECTION * SLAB_ROWS, D)
    return (new_master, new_first, new_second, checkpoint, weights_new, hidden_grad)
```

```python
import jax
import jax.numpy as jnp
from jax import lax
from jax.experimental import pallas as pl
from jax.experimental.pallas import tpu as pltpu
from jax.sharding import PartitionSpec as P

MESH = pl.DeviceIdType.MESH
F32 = jnp.float32
BF16 = jnp.bfloat16

D = 6144
ROWS = 64
TOK = 256
CH = 3
W = D // CH
J = W // 128
FLIPS = [(i, f) for f in (1, 0) for i in range(4) if (i, f) != (0, 0)]


def rep_of(p):
    c, xh, zl, zh = p // 32, (p // 16) % 2, (p // 4) % 4, p % 4
    return (zh * 4 + zl) * 4 + xh * 2 + c


def kernel(
    hid_hbm, own_hbm, step_ref, og_hbm, w_hbm, m_hbm, f_hbm, s_hbm,
    nm_ref, nf_ref, ns_ref, ck_ref, wn_ref, hg_ref,
    hid_ref, own_ref, m_ref, f_ref, s_ref, og, w, part, core_in, full, t1, in1, acc1, t2, in2, ag, wide, moved,
    ld_sem, core_s, core_r, s1, r1, s2, r2, sa, ra, sb, rb, sc, rc, sk, rk,
):
    r = lax.axis_index("replica")
    z, xh, c = r // 4, (r // 2) % 2, r % 2
    a, zl = z // 4, z % 4
    g = xh * 4 + zl

    def rep(z_, x_, c_):
        return ((z_ + 32) % 16) * 4 + x_ * 2 + c_

    offs = [0, 1, -1, 2 - 4 * c]
    sib = rep(z, xh, 1 - c)
    nxt, prv = (r + 1) % 64, (r + 63) % 64
    near_to = [(rep(z + offs[i], (xh + f) % 2, c)) for i, f in FLIPS]
    near_from = [(rep(z - offs[i], (xh + f) % 2, c)) for i, f in FLIPS]
    far = [rep(z + 4 * d, xh, c) for d in (1, 2, 3)]

    def remote(src, dst, ssem, rsem, to):
        return pltpu.make_async_remote_copy(
            src_ref=src, dst_ref=dst, send_sem=ssem, recv_sem=rsem,
            device_id={"replica": to}, device_id_type=MESH,
        )

    loads = [
        pltpu.make_async_copy(own_hbm, own_ref, ld_sem.at[CH + 1]),
        pltpu.make_async_copy(hid_hbm, hid_ref, ld_sem.at[CH + 2]),
    ]
    for ch in range(CH):
        cols = pl.ds(ch * W, W)
        loads.append(pltpu.make_async_copy(og_hbm.at[:, cols], og.at[:, cols], ld_sem.at[ch]))
    loads += [
        pltpu.make_async_copy(w_hbm, w, ld_sem.at[CH]),
        pltpu.make_async_copy(m_hbm, m_ref, ld_sem.at[CH + 3]),
        pltpu.make_async_copy(f_hbm, f_ref, ld_sem.at[CH + 4]),
        pltpu.make_async_copy(s_hbm, s_ref, ld_sem.at[CH + 5]),
    ]
    for x in loads:
        x.start()

    barrier = pltpu.get_barrier_semaphore()
    for to in [sib, prv] + near_from + far:
        pl.semaphore_signal(barrier, inc=1, device_id={"replica": to}, device_id_type=MESH)

    loads[0].wait()
    loads[1].wait()
    k_i = lax.broadcasted_iota(jnp.int32, (ROWS, ROWS), 0)
    p_i = lax.broadcasted_iota(jnp.int32, (ROWS, ROWS), 1)
    owns = jnp.where(own_ref[...] == k_i, 1.0, 0.0).astype(BF16)
    places = jnp.where(k_i == rep_of(p_i), 1.0, 0.0).astype(BF16)
    at = jnp.dot(owns, places, preferred_element_type=F32).astype(BF16)
    hid = lax.dot_general(
        at, hid_ref[...], (((0,), (0,)), ((), ())), preferred_element_type=F32
    ).astype(BF16)

    sends = []

    def start(copy):
        copy.start()
        sends.append(copy)
        return copy

    mine = pl.ds(pl.multiple_of(c * 32, 32), 32)
    theirs = pl.ds(pl.multiple_of((1 - c) * 32, 32), 32)
    core = []
    for ch in range(CH):
        loads[2 + ch].wait()
        for n in range(W // 512):
            at_col = ch * W + n * 512
            part[ch, :, n * 512 : (n + 1) * 512] = jnp.dot(
                hid, og[:, at_col : at_col + 512], preferred_element_type=F32
            )
        if ch == 0:
            pl.semaphore_wait(barrier, 12)
        core.append(
            start(remote(part.at[ch, theirs], core_in.at[ch], core_s.at[ch], core_r.at[ch], sib))
        )

    near = []
    for ch in range(CH):
        core[ch].wait_recv()
        for j in range(J):
            lanes = pl.ds(j * 128, 128)
            full[ch, pl.ds(j, 32, stride=J), :] = part[ch, mine, lanes] + core_in[ch, :, lanes]
        t1[ch] = full[ch].astype(BF16)
        row = []
        for k, (i, f) in enumerate(FLIPS):
            there = ((xh + f) % 2) * 4 + (z + offs[i] + 16) % 4
            src = t1.at[ch, pl.ds(pl.multiple_of(there * 4 * J, 64), 4 * J)]
            row.append(start(remote(src, in1.at[ch, k], s1.at[ch, k], r1.at[ch, k], near_to[k])))
        near.append(row)

    loads[2 + CH].wait()

    def back_step(n, total):
        cols = pl.ds(pl.multiple_of(n * 512, 512), 512)
        return total + lax.dot_general(
            w[:, cols], og[:, cols], (((1,), (1,)), ((), ())), preferred_element_type=F32
        )

    back = lax.fori_loop(0, D // 512, back_step, jnp.zeros((ROWS, TOK), F32))
    hg_ref[...] = (back * D ** (-0.5)).astype(BF16)

    group = pl.ds(pl.multiple_of(g * 4 * J, 64), 4 * J)
    far_c = []
    for ch in range(CH):
        total = full[ch, group, :]
        for k in range(7):
            near[ch][k].wait_recv()
            total = total + in1[ch, k].astype(F32)
        acc1[ch] = total
        t2[ch] = total.astype(BF16)
        row = []
        for d in (1, 2, 3):
            src = t2.at[ch, pl.ds(pl.multiple_of(((a + d) % 4) * J, J), J)]
            row.append(
                start(remote(src, in2.at[ch, d - 1], s2.at[ch, d - 1], r2.at[ch, d - 1], far[d - 1]))
            )
        far_c.append(row)

    steps = jnp.full((J, 128), step_ref[0], jnp.int32)
    pow1 = jnp.full((J, 128), 1.0, F32)
    pow2 = pow1
    for n in range(1, 9):
        pow1 = pow1 * jnp.where(steps >= n, 0.9, 1.0).astype(F32)
        pow2 = pow2 * jnp.where(steps >= n, 0.95, 1.0).astype(F32)
    fix1, fix2 = 1.0 - pow1, 1.0 - pow2

    own_rows = pl.ds(pl.multiple_of((c * 32 + g * 4 + a) * J, J), J)
    for x in loads[3 + CH :]:
        x.wait()
    first_c = []
    for ch in range(CH):
        grads = acc1[ch, pl.ds(pl.multiple_of(a * J, J), J), :]
        for d in range(3):
            far_c[ch][d].wait_recv()
            grads = grads + in2[ch, d].astype(F32)
        grads = grads * (1.0 / TOK)
        at_rows = pl.ds(ch * J, J)
        master = m_ref[at_rows, :]
        new_f = 0.9 * f_ref[at_rows, :] + 0.1 * grads
        new_s = 0.95 * s_ref[at_rows, :] + 0.05 * grads * grads
        update = new_f / fix1 / (jnp.sqrt(new_s / fix2) + 1e-08)
        new_m = master - 0.05 * (update + 0.1 * master)
        ag[ch, own_rows, :] = new_m.astype(BF16)
        row = []
        for d in range(3):
            here = ag.at[ch, own_rows]
            row.append(start(remote(here, here, sa.at[ch, d], ra.at[ch, d], far[d])))
        first_c.append(row)
        nm_ref[at_rows, :] = new_m
        nf_ref[at_rows, :] = new_f
        ns_ref[at_rows, :] = new_s
        moved[0, at_rows, :] = new_m
        moved[1, at_rows, :] = new_f
        moved[2, at_rows, :] = new_s

    mine_g = pl.ds(pl.multiple_of((c * 8 + g) * 4 * J, 64), 4 * J)
    second_c = []
    for ch in range(CH):
        for d in range(3):
            first_c[ch][d].wait_recv()
        row = []
        for k in range(7):
            here = ag.at[ch, mine_g]
            row.append(start(remote(here, here, sb.at[ch, k], rb.at[ch, k], near_to[k])))
        second_c.append(row)
    ck = start(remote(moved, ck_ref, sk, rk, nxt))

    half = pl.ds(pl.multiple_of(c * 32 * J, 512), 32 * J)
    third_c = []
    for ch in range(CH):
        for k in range(7):
            second_c[ch][k].wait_recv()
        here = ag.at[ch, half]
        third_c.append(start(remote(here, here, sc.at[ch], rc.at[ch], sib)))
    for ch in range(CH):
        third_c[ch].wait_recv()
        wide[ch] = ag[ch].astype(F32)
        for n in range(J // 4):
            rows = [
                wide[ch, pl.ds(4 * n + q, ROWS, stride=J), :].astype(BF16) for q in range(4)
            ]
            wn_ref[:, pl.ds(ch * W + n * 512, 512)] = jnp.dot(
                at, jnp.concatenate(rows, axis=1), preferred_element_type=F32
            ).astype(BF16)
    ck.wait_recv()
    for copy in sends:
        copy.wait_send()


def per_device(
    hidden, out_grad, weights_old, master, first_moment, second_moment, owner_order, step_count
):
    vmem = pl.BlockSpec(memory_space=pltpu.VMEM)
    hbm = pl.BlockSpec(memory_space=pltpu.HBM)
    own = jax.ShapeDtypeStruct((48, 128), F32)
    dma = pltpu.SemaphoreType.DMA
    nm, nf, ns, ck, wn, hg = pl.pallas_call(
        kernel,
        out_shape=(
            own, own, own,
            jax.ShapeDtypeStruct((3, 48, 128), F32),
            jax.ShapeDtypeStruct((ROWS, D), BF16),
            jax.ShapeDtypeStruct((ROWS, TOK), BF16),
        ),
        in_specs=[
            hbm, hbm, pl.BlockSpec(memory_space=pltpu.SMEM), hbm, hbm, hbm, hbm, hbm,
        ],
        out_specs=(vmem,) * 6,
        scratch_shapes=[
            pltpu.VMEM((ROWS, TOK), BF16),
            pltpu.VMEM((1, ROWS), jnp.int32),
            pltpu.VMEM((48, 128), F32),
            pltpu.VMEM((48, 128), F32),
            pltpu.VMEM((48, 128), F32),
            pltpu.VMEM((TOK, D), BF16),
            pltpu.VMEM((ROWS, D), BF16),
            pltpu.VMEM((CH, ROWS, W), F32),
            pltpu.VMEM((CH, 32, W), F32),
            pltpu.VMEM((CH, 32 * J, 128), F32),
            pltpu.VMEM((CH, 32 * J, 128), BF16),
            pltpu.VMEM((CH, 7, 4 * J, 128), BF16),
            pltpu.VMEM((CH, 4 * J, 128), F32),
            pltpu.VMEM((CH, 4 * J, 128), BF16),
            pltpu.VMEM((CH, 3, J, 128), BF16),
            pltpu.VMEM((CH, 64 * J, 128), BF16),
            pltpu.VMEM((CH, 64 * J, 128), F32),
            pltpu.VMEM((3, 48, 128), F32),
            dma((CH + 6,)),
            dma((CH,)), dma((CH,)),
            dma((CH, 7)), dma((CH, 7)),
            dma((CH, 3)), dma((CH, 3)),
            dma((CH, 3)), dma((CH, 3)),
            dma((CH, 7)), dma((CH, 7)),
            dma((CH,)), dma((CH,)),
            dma, dma,
        ],
        compiler_params=pltpu.CompilerParams(
            collective_id=0, has_side_effects=True, vmem_limit_bytes=60 * 1024 * 1024
        ),
        cost_estimate=pl.CostEstimate(
            flops=4 * ROWS * TOK * D, bytes_accessed=6 * 1024 * 1024, transcendentals=0
        ),
    )(
        hidden[0].T,
        owner_order.reshape(1, ROWS),
        step_count,
        out_grad[0],
        weights_old,
        master.reshape(48, 128),
        first_moment.reshape(48, 128),
        second_moment.reshape(48, 128),
    )
    return (
        nm.reshape(1, D), nf.reshape(1, D), ns.reshape(1, D),
        ck.reshape(3, 1, D), wn, hg.T[None],
    )


def solution(mesh):
    placed = (
        P("section", "replica", None),
        P("section", "replica", None),
        P("section", None),
        P(("section", "replica"), None),
        P(("section", "replica"), None),
        P(("section", "replica"), None),
        P(),
        P(),
    )
    return jax.shard_map(
        per_device,
        mesh=mesh,
        in_specs=placed,
        out_specs=(
            P(("section", "replica"), None),
            P(("section", "replica"), None),
            P(("section", "replica"), None),
            P(None, ("section", "replica"), None),
            P("section", None),
            P("section", "replica", None),
        ),
        check_vma=False,
    )
```

```python
import jax
import jax.numpy as jnp
from jax import lax
from jax.experimental import pallas as pl
from jax.experimental.pallas import tpu as pltpu
from jax.sharding import PartitionSpec as P

MESH = pl.DeviceIdType.MESH
F32 = jnp.float32
BF16 = jnp.bfloat16

D = 6144
ROWS = 64
TOK = 256
CH = 3
W = D // CH
J = W // 128
FLIPS = [(i, f) for f in (1, 0) for i in range(4) if (i, f) != (0, 0)]


def rep_of(p):
    c, xh, zl, zh = p // 32, (p // 16) % 2, (p // 4) % 4, p % 4
    return (zh * 4 + zl) * 4 + xh * 2 + c


def kernel(
    hid_hbm, own_hbm, step_ref, og_hbm, w_hbm, m_hbm, f_hbm, s_hbm,
    nm_ref, nf_ref, ns_ref, ck_ref, wn_ref, hg_ref,
    hid_ref, own_ref, m_ref, f_ref, s_ref, og, w, part, core_in, full, t1, in1, acc1, t2, in2, ag, wide, moved,
    ld_sem, core_s, core_r, s1, r1, s2, r2, sa, ra, sb, rb, sc, rc, sk, rk,
):
    r = lax.axis_index("replica")
    z, xh, c = r // 4, (r // 2) % 2, r % 2
    a, zl = z // 4, z % 4
    g = xh * 4 + zl

    def rep(z_, x_, c_):
        return ((z_ + 32) % 16) * 4 + x_ * 2 + c_

    offs = [0, 1, -1, 2 - 4 * c]
    sib = rep(z, xh, 1 - c)
    nxt, prv = (r + 1) % 64, (r + 63) % 64
    near_to = [(rep(z + offs[i], (xh + f) % 2, c)) for i, f in FLIPS]
    near_from = [(rep(z - offs[i], (xh + f) % 2, c)) for i, f in FLIPS]
    far = [rep(z + 4 * d, xh, c) for d in (1, 2, 3)]

    def remote(src, dst, ssem, rsem, to):
        return pltpu.make_async_remote_copy(
            src_ref=src, dst_ref=dst, send_sem=ssem, recv_sem=rsem,
            device_id={"replica": to}, device_id_type=MESH,
        )

    loads = [
        pltpu.make_async_copy(own_hbm, own_ref, ld_sem.at[CH + 1]),
        pltpu.make_async_copy(hid_hbm, hid_ref, ld_sem.at[CH + 2]),
    ]
    for ch in range(CH):
        cols = pl.ds(ch * W, W)
        loads.append(pltpu.make_async_copy(og_hbm.at[:, cols], og.at[:, cols], ld_sem.at[ch]))
    loads += [
        pltpu.make_async_copy(w_hbm, w, ld_sem.at[CH]),
        pltpu.make_async_copy(m_hbm, m_ref, ld_sem.at[CH + 3]),
        pltpu.make_async_copy(f_hbm, f_ref, ld_sem.at[CH + 4]),
        pltpu.make_async_copy(s_hbm, s_ref, ld_sem.at[CH + 5]),
    ]
    for x in loads:
        x.start()

    barrier = pltpu.get_barrier_semaphore()
    for to in [sib, prv] + near_from + far:
        pl.semaphore_signal(barrier, inc=1, device_id={"replica": to}, device_id_type=MESH)

    loads[0].wait()
    loads[1].wait()
    k_i = lax.broadcasted_iota(jnp.int32, (ROWS, ROWS), 0)
    p_i = lax.broadcasted_iota(jnp.int32, (ROWS, ROWS), 1)
    owns = jnp.where(own_ref[...] == k_i, 1.0, 0.0).astype(BF16)
    places = jnp.where(k_i == rep_of(p_i), 1.0, 0.0).astype(BF16)
    at = jnp.dot(owns, places, preferred_element_type=F32).astype(BF16)
    hid = lax.dot_general(
        at, hid_ref[...], (((0,), (0,)), ((), ())), preferred_element_type=F32
    ).astype(BF16)

    sends = []

    def start(copy):
        copy.start()
        sends.append(copy)
        return copy

    mine = pl.ds(pl.multiple_of(c * 32, 32), 32)
    theirs = pl.ds(pl.multiple_of((1 - c) * 32, 32), 32)
    core = []
    for ch in range(CH):
        loads[2 + ch].wait()
        for n in range(W // 512):
            at_col = ch * W + n * 512
            part[ch, :, n * 512 : (n + 1) * 512] = jnp.dot(
                hid, og[:, at_col : at_col + 512], preferred_element_type=F32
            )
        if ch == 0:
            pl.semaphore_wait(barrier, 12)
        core.append(
            start(remote(part.at[ch, theirs], core_in.at[ch], core_s.at[ch], core_r.at[ch], sib))
        )

    near = []
    for ch in range(CH):
        core[ch].wait_recv()
        for j in range(J):
            lanes = pl.ds(j * 128, 128)
            full[ch, pl.ds(j, 32, stride=J), :] = part[ch, mine, lanes] + core_in[ch, :, lanes]
        t1[ch] = full[ch].astype(BF16)
        row = []
        for k, (i, f) in enumerate(FLIPS):
            there = ((xh + f) % 2) * 4 + (z + offs[i] + 16) % 4
            src = t1.at[ch, pl.ds(pl.multiple_of(there * 4 * J, 64), 4 * J)]
            row.append(start(remote(src, in1.at[ch, k], s1.at[ch, k], r1.at[ch, k], near_to[k])))
        near.append(row)

    loads[2 + CH].wait()

    def back_step(n, total):
        cols = pl.ds(pl.multiple_of(n * 512, 512), 512)
        return total + lax.dot_general(
            w[:, cols], og[:, cols], (((1,), (1,)), ((), ())), preferred_element_type=F32
        )

    back = lax.fori_loop(0, D // 512, back_step, jnp.zeros((ROWS, TOK), F32))
    hg_ref[...] = (back * D ** (-0.5)).astype(BF16)

    group = pl.ds(pl.multiple_of(g * 4 * J, 64), 4 * J)
    far_c = []
    for ch in range(CH):
        total = full[ch, group, :]
        for k in range(7):
            near[ch][k].wait_recv()
            total = total + in1[ch, k].astype(F32)
        acc1[ch] = total
        t2[ch] = total.astype(BF16)
        row = []
        for d in (1, 2, 3):
            src = t2.at[ch, pl.ds(pl.multiple_of(((a + d) % 4) * J, J), J)]
            row.append(
                start(remote(src, in2.at[ch, d - 1], s2.at[ch, d - 1], r2.at[ch, d - 1], far[d - 1]))
            )
        far_c.append(row)

    steps = jnp.full((J, 128), step_ref[0], jnp.int32)
    pow1 = jnp.full((J, 128), 1.0, F32)
    pow2 = pow1
    for n in range(1, 9):
        pow1 = pow1 * jnp.where(steps >= n, 0.9, 1.0).astype(F32)
        pow2 = pow2 * jnp.where(steps >= n, 0.95, 1.0).astype(F32)
    fix1, fix2 = 1.0 - pow1, 1.0 - pow2

    own_rows = pl.ds(pl.multiple_of((c * 32 + g * 4 + a) * J, J), J)
    for x in loads[3 + CH :]:
        x.wait()
    first_c = []
    for ch in range(CH):
        grads = acc1[ch, pl.ds(pl.multiple_of(a * J, J), J), :]
        for d in range(3):
            far_c[ch][d].wait_recv()
            grads = grads + in2[ch, d].astype(F32)
        grads = grads * (1.0 / TOK)
        at_rows = pl.ds(ch * J, J)
        master = m_ref[at_rows, :]
        new_f = 0.9 * f_ref[at_rows, :] + 0.1 * grads
        new_s = 0.95 * s_ref[at_rows, :] + 0.05 * grads * grads
        update = new_f / fix1 / (jnp.sqrt(new_s / fix2) + 1e-08)
        new_m = master - 0.05 * (update + 0.1 * master)
        ag[ch, own_rows, :] = new_m.astype(BF16)
        row = []
        for d in range(3):
            here = ag.at[ch, own_rows]
            row.append(start(remote(here, here, sa.at[ch, d], ra.at[ch, d], far[d])))
        first_c.append(row)
        nm_ref[at_rows, :] = new_m
        nf_ref[at_rows, :] = new_f
        ns_ref[at_rows, :] = new_s
        moved[0, at_rows, :] = new_m
        moved[1, at_rows, :] = new_f
        moved[2, at_rows, :] = new_s

    mine_g = pl.ds(pl.multiple_of((c * 8 + g) * 4 * J, 64), 4 * J)
    second_c = []
    for ch in range(CH):
        for d in range(3):
            first_c[ch][d].wait_recv()
        row = []
        for k in range(7):
            here = ag.at[ch, mine_g]
            row.append(start(remote(here, here, sb.at[ch, k], rb.at[ch, k], near_to[k])))
        second_c.append(row)
    ck = start(remote(moved, ck_ref, sk, rk, nxt))

    half = pl.ds(pl.multiple_of(c * 32 * J, 512), 32 * J)
    third_c = []
    for ch in range(CH):
        for k in range(7):
            second_c[ch][k].wait_recv()
        here = ag.at[ch, half]
        third_c.append(start(remote(here, here, sc.at[ch], rc.at[ch], sib)))
    other = pl.ds(pl.multiple_of((1 - c) * 32 * J, 512), 32 * J)
    for ch in range(CH):
        wide[ch, half, :] = ag[ch, half, :].astype(F32)
    for ch in range(CH):
        third_c[ch].wait_recv()
        wide[ch, other, :] = ag[ch, other, :].astype(F32)
        for n in range(J // 4):
            rows = [
                wide[ch, pl.ds(4 * n + q, ROWS, stride=J), :].astype(BF16) for q in range(4)
            ]
            wn_ref[:, pl.ds(ch * W + n * 512, 512)] = jnp.dot(
                at, jnp.concatenate(rows, axis=1), preferred_element_type=F32
            ).astype(BF16)
    ck.wait_recv()
    for copy in sends:
        copy.wait_send()


def write_out(*refs):
    srcs, dsts, sems = refs[:6], refs[6:12], refs[12]
    copies = [pltpu.make_async_copy(a, b, sems.at[i]) for i, (a, b) in enumerate(zip(srcs, dsts))]
    for x in copies:
        x.start()
    for x in copies:
        x.wait()


def per_device(
    hidden, out_grad, weights_old, master, first_moment, second_moment, owner_order, step_count
):
    vmem = pl.BlockSpec(memory_space=pltpu.VMEM)
    hbm = pl.BlockSpec(memory_space=pltpu.HBM)
    own = pltpu.VMEM((48, 128), F32)
    dma = pltpu.SemaphoreType.DMA
    nm, nf, ns, ck, wn, hg = pl.pallas_call(
        kernel,
        out_shape=(
            own, own, own,
            pltpu.VMEM((3, 48, 128), F32),
            pltpu.VMEM((ROWS, D), BF16),
            pltpu.VMEM((ROWS, TOK), BF16),
        ),
        in_specs=[
            hbm, hbm, pl.BlockSpec(memory_space=pltpu.SMEM), hbm, hbm, hbm, hbm, hbm,
        ],
        out_specs=(vmem,) * 6,
        scratch_shapes=[
            pltpu.VMEM((ROWS, TOK), BF16),
            pltpu.VMEM((1, ROWS), jnp.int32),
            pltpu.VMEM((48, 128), F32),
            pltpu.VMEM((48, 128), F32),
            pltpu.VMEM((48, 128), F32),
            pltpu.VMEM((TOK, D), BF16),
            pltpu.VMEM((ROWS, D), BF16),
            pltpu.VMEM((CH, ROWS, W), F32),
            pltpu.VMEM((CH, 32, W), F32),
            pltpu.VMEM((CH, 32 * J, 128), F32),
            pltpu.VMEM((CH, 32 * J, 128), BF16),
            pltpu.VMEM((CH, 7, 4 * J, 128), BF16),
            pltpu.VMEM((CH, 4 * J, 128), F32),
            pltpu.VMEM((CH, 4 * J, 128), BF16),
            pltpu.VMEM((CH, 3, J, 128), BF16),
            pltpu.VMEM((CH, 64 * J, 128), BF16),
            pltpu.VMEM((CH, 64 * J, 128), F32),
            pltpu.VMEM((3, 48, 128), F32),
            dma((CH + 6,)),
            dma((CH,)), dma((CH,)),
            dma((CH, 7)), dma((CH, 7)),
            dma((CH, 3)), dma((CH, 3)),
            dma((CH, 3)), dma((CH, 3)),
            dma((CH, 7)), dma((CH, 7)),
            dma((CH,)), dma((CH,)),
            dma, dma,
        ],
        compiler_params=pltpu.CompilerParams(
            collective_id=0, has_side_effects=True, vmem_limit_bytes=60 * 1024 * 1024
        ),
        cost_estimate=pl.CostEstimate(
            flops=4 * ROWS * TOK * D, bytes_accessed=6 * 1024 * 1024, transcendentals=0
        ),
    )(
        hidden[0].T,
        owner_order.reshape(1, ROWS),
        step_count,
        out_grad[0],
        weights_old,
        master.reshape(48, 128),
        first_moment.reshape(48, 128),
        second_moment.reshape(48, 128),
    )
    nm, nf, ns, ck, wn, hg = pl.pallas_call(
        write_out,
        out_shape=[jax.ShapeDtypeStruct(x.shape, x.dtype) for x in (nm, nf, ns, ck, wn, hg)],
        in_specs=[vmem] * 6,
        out_specs=[hbm] * 6,
        scratch_shapes=[dma((6,))],
        compiler_params=pltpu.CompilerParams(vmem_limit_bytes=2 * 1024 * 1024),
    )(nm, nf, ns, ck, wn, hg)
    return (
        nm.reshape(1, D), nf.reshape(1, D), ns.reshape(1, D),
        ck.reshape(3, 1, D), wn, hg.T[None],
    )


def solution(mesh):
    placed = (
        P("section", "replica", None),
        P("section", "replica", None),
        P("section", None),
        P(("section", "replica"), None),
        P(("section", "replica"), None),
        P(("section", "replica"), None),
        P(),
        P(),
    )
    return jax.shard_map(
        per_device,
        mesh=mesh,
        in_specs=placed,
        out_specs=(
            P(("section", "replica"), None),
            P(("section", "replica"), None),
            P(("section", "replica"), None),
            P(None, ("section", "replica"), None),
            P("section", None),
            P("section", "replica", None),
        ),
        check_vma=False,
    )
```

```python
import jax
import jax.numpy as jnp
from jax import lax
from jax.experimental import pallas as pl
from jax.experimental.pallas import tpu as pltpu
from jax.sharding import PartitionSpec as P

MESH = pl.DeviceIdType.MESH
F32 = jnp.float32
BF16 = jnp.bfloat16

D = 6144
ROWS = 64
TOK = 256
CH = 3
W = D // CH
J = W // 128
FAR = (6, -6, 2, -2)
FLIPS = [(i, f) for f in (1, 0) for i in range(4) if (i, f) != (0, 0)]


def rep_of(p):
    c, xh, zl, zh = p // 32, (p // 16) % 2, (p // 4) % 4, p % 4
    return (zh * 4 + zl) * 4 + xh * 2 + c


def kernel(
    hid_hbm, own_hbm, step_ref, og_hbm, w_hbm, m_hbm, f_hbm, s_hbm,
    nm_ref, nf_ref, ns_ref, ck_ref, wn_ref, hg_ref,
    hid_ref, own_ref, m_ref, f_ref, s_ref, og, w, part, core_in, full, t1, in1, t2, in2, fresh, ag, wide, moved,
    ld_sem, core_s, core_r, s1, r1, s2, r2, sa, ra, sb, rb, sc, rc, sk, rk,
):
    r = lax.axis_index("replica")
    z, xh, c = r // 4, (r // 2) % 2, r % 2
    a, zl = z // 4, z % 4
    g = xh * 4 + (z + 2) % 4

    def rep(z_, x_, c_):
        return ((z_ + 32) % 16) * 4 + x_ * 2 + c_

    offs = [0, 1, -1, 2 - 4 * c]
    sib = rep(z, xh, 1 - c)
    nxt, prv = (r + 1) % 64, (r + 63) % 64
    near_to = [(rep(z + offs[i], (xh + f) % 2, c)) for i, f in FLIPS]
    near_from = [(rep(z - offs[i], (xh + f) % 2, c)) for i, f in FLIPS]
    far = [rep(z + d, xh, c) for d in FAR]

    def remote(src, dst, ssem, rsem, to):
        return pltpu.make_async_remote_copy(
            src_ref=src, dst_ref=dst, send_sem=ssem, recv_sem=rsem,
            device_id={"replica": to}, device_id_type=MESH,
        )

    loads = [
        pltpu.make_async_copy(own_hbm, own_ref, ld_sem.at[CH + 1]),
        pltpu.make_async_copy(hid_hbm, hid_ref, ld_sem.at[CH + 2]),
    ]
    for ch in range(CH):
        cols = pl.ds(ch * W, W)
        loads.append(pltpu.make_async_copy(og_hbm.at[:, cols], og.at[:, cols], ld_sem.at[ch]))
    loads += [
        pltpu.make_async_copy(w_hbm, w, ld_sem.at[CH]),
        pltpu.make_async_copy(m_hbm, m_ref, ld_sem.at[CH + 3]),
        pltpu.make_async_copy(f_hbm, f_ref, ld_sem.at[CH + 4]),
        pltpu.make_async_copy(s_hbm, s_ref, ld_sem.at[CH + 5]),
    ]
    for x in loads:
        x.start()

    barrier = pltpu.get_barrier_semaphore()
    for to in [sib, prv] + near_from + far:
        pl.semaphore_signal(barrier, inc=1, device_id={"replica": to}, device_id_type=MESH)

    loads[0].wait()
    loads[1].wait()
    k_i = lax.broadcasted_iota(jnp.int32, (ROWS, ROWS), 0)
    p_i = lax.broadcasted_iota(jnp.int32, (ROWS, ROWS), 1)
    owns = jnp.where(own_ref[...] == k_i, 1.0, 0.0).astype(BF16)
    places = jnp.where(k_i == rep_of(p_i), 1.0, 0.0).astype(BF16)
    at = jnp.dot(owns, places, preferred_element_type=F32).astype(BF16)
    hid = lax.dot_general(
        at, hid_ref[...], (((0,), (0,)), ((), ())), preferred_element_type=F32
    ).astype(BF16)

    sends = []

    def start(copy):
        copy.start()
        sends.append(copy)
        return copy

    mine = pl.ds(pl.multiple_of(c * 32, 32), 32)
    theirs = pl.ds(pl.multiple_of((1 - c) * 32, 32), 32)
    core = []
    for ch in range(CH):
        loads[2 + ch].wait()
        for n in range(W // 512):
            at_col = ch * W + n * 512
            part[ch, :, n * 512 : (n + 1) * 512] = jnp.dot(
                hid, og[:, at_col : at_col + 512], preferred_element_type=F32
            )
        if ch == 0:
            pl.semaphore_wait(barrier, 13)
        core.append(
            start(remote(part.at[ch, theirs], core_in.at[ch], core_s.at[ch], core_r.at[ch], sib))
        )

    near = []
    for ch in range(CH):
        core[ch].wait_recv()
        for j in range(J):
            lanes = pl.ds(j * 128, 128)
            full[ch, pl.ds(j, 32, stride=J), :] = part[ch, mine, lanes] + core_in[ch, :, lanes]
        t1[ch] = full[ch].astype(BF16)
        row = []
        for k, (i, f) in enumerate(FLIPS):
            there = ((xh + f) % 2) * 4 + (z + offs[i] + 18) % 4
            src = t1.at[ch, pl.ds(pl.multiple_of(there * 4 * J, 64), 4 * J)]
            row.append(start(remote(src, in1.at[ch, k], s1.at[ch, k], r1.at[ch, k], near_to[k])))
        near.append(row)

    loads[2 + CH].wait()

    def back_step(n, total):
        cols = pl.ds(pl.multiple_of(n * 512, 512), 512)
        return total + lax.dot_general(
            w[:, cols], og[:, cols], (((1,), (1,)), ((), ())), preferred_element_type=F32
        )

    back = lax.fori_loop(0, D // 512, back_step, jnp.zeros((ROWS, TOK), F32))
    hg_ref[...] = (back * D ** (-0.5)).astype(BF16)

    group = pl.ds(pl.multiple_of(g * 4 * J, 64), 4 * J)
    far_c = []
    for ch in range(CH):
        total = full[ch, group, :]
        for k in range(7):
            near[ch][k].wait_recv()
            total = total + in1[ch, k].astype(F32)
        t2[ch] = total.astype(BF16)
        row = []
        for d in range(4):
            block = ((z + FAR[d] + 16) % 16) // 4
            src = t2.at[ch, pl.ds(pl.multiple_of(block * J, J), J)]
            row.append(start(remote(src, in2.at[ch, d], s2.at[ch, d], r2.at[ch, d], far[d])))
        far_c.append(row)

    steps = jnp.full((J, 128), step_ref[0], jnp.int32)
    pow1 = jnp.full((J, 128), 1.0, F32)
    pow2 = pow1
    for n in range(1, 9):
        pow1 = pow1 * jnp.where(steps >= n, 0.9, 1.0).astype(F32)
        pow2 = pow2 * jnp.where(steps >= n, 0.95, 1.0).astype(F32)
    fix1, fix2 = 1.0 - pow1, 1.0 - pow2

    own_rows = pl.ds(pl.multiple_of((c * 32 + xh * 16 + zl * 4 + a) * J, J), J)
    for x in loads[3 + CH :]:
        x.wait()
    first_c = []
    for ch in range(CH):
        for d in range(4):
            far_c[ch][d].wait_recv()
        grads = in2[ch, 0].astype(F32) + in2[ch, 1].astype(F32)
        grads = grads + in2[ch, 2].astype(F32) + in2[ch, 3].astype(F32)
        grads = grads * (1.0 / TOK)
        at_rows = pl.ds(ch * J, J)
        master = m_ref[at_rows, :]
        new_f = 0.9 * f_ref[at_rows, :] + 0.1 * grads
        new_s = 0.95 * s_ref[at_rows, :] + 0.05 * grads * grads
        update = new_f / fix1 / (jnp.sqrt(new_s / fix2) + 1e-08)
        new_m = master - 0.05 * (update + 0.1 * master)
        fresh[ch] = new_m.astype(BF16)
        row = []
        for d in range(4):
            there = ag.at[ch, own_rows]
            row.append(start(remote(fresh.at[ch], there, sa.at[ch, d], ra.at[ch, d], far[d])))
        first_c.append(row)
        nm_ref[at_rows, :] = new_m
        nf_ref[at_rows, :] = new_f
        ns_ref[at_rows, :] = new_s
        moved[0, at_rows, :] = new_m
        moved[1, at_rows, :] = new_f
        moved[2, at_rows, :] = new_s

    mine_g = pl.ds(pl.multiple_of((c * 8 + g) * 4 * J, 64), 4 * J)
    second_c = []
    for ch in range(CH):
        for d in range(4):
            first_c[ch][d].wait_recv()
        row = []
        for k in range(7):
            here = ag.at[ch, mine_g]
            row.append(start(remote(here, here, sb.at[ch, k], rb.at[ch, k], near_to[k])))
        second_c.append(row)
    ck = start(remote(moved, ck_ref, sk, rk, nxt))

    half = pl.ds(pl.multiple_of(c * 32 * J, 512), 32 * J)
    third_c = []
    for ch in range(CH):
        for k in range(7):
            second_c[ch][k].wait_recv()
        here = ag.at[ch, half]
        third_c.append(start(remote(here, here, sc.at[ch], rc.at[ch], sib)))
    other = pl.ds(pl.multiple_of((1 - c) * 32 * J, 512), 32 * J)
    for ch in range(CH):
        wide[ch, half, :] = ag[ch, half, :].astype(F32)
    for ch in range(CH):
        third_c[ch].wait_recv()
        wide[ch, other, :] = ag[ch, other, :].astype(F32)
        for n in range(J // 4):
            rows = [
                wide[ch, pl.ds(4 * n + q, ROWS, stride=J), :].astype(BF16) for q in range(4)
            ]
            wn_ref[:, pl.ds(ch * W + n * 512, 512)] = jnp.dot(
                at, jnp.concatenate(rows, axis=1), preferred_element_type=F32
            ).astype(BF16)
    ck.wait_recv()
    for copy in sends:
        copy.wait_send()


def write_out(*refs):
    srcs, dsts, sems = refs[:6], refs[6:12], refs[12]
    copies = [pltpu.make_async_copy(a, b, sems.at[i]) for i, (a, b) in enumerate(zip(srcs, dsts))]
    for x in copies:
        x.start()
    for x in copies:
        x.wait()


def per_device(
    hidden, out_grad, weights_old, master, first_moment, second_moment, owner_order, step_count
):
    vmem = pl.BlockSpec(memory_space=pltpu.VMEM)
    hbm = pl.BlockSpec(memory_space=pltpu.HBM)
    own = pltpu.VMEM((48, 128), F32)
    dma = pltpu.SemaphoreType.DMA
    nm, nf, ns, ck, wn, hg = pl.pallas_call(
        kernel,
        out_shape=(
            own, own, own,
            pltpu.VMEM((3, 48, 128), F32),
            pltpu.VMEM((ROWS, D), BF16),
            pltpu.VMEM((ROWS, TOK), BF16),
        ),
        in_specs=[
            hbm, hbm, pl.BlockSpec(memory_space=pltpu.SMEM), hbm, hbm, hbm, hbm, hbm,
        ],
        out_specs=(vmem,) * 6,
        scratch_shapes=[
            pltpu.VMEM((ROWS, TOK), BF16),
            pltpu.VMEM((1, ROWS), jnp.int32),
            pltpu.VMEM((48, 128), F32),
            pltpu.VMEM((48, 128), F32),
            pltpu.VMEM((48, 128), F32),
            pltpu.VMEM((TOK, D), BF16),
            pltpu.VMEM((ROWS, D), BF16),
            pltpu.VMEM((CH, ROWS, W), F32),
            pltpu.VMEM((CH, 32, W), F32),
            pltpu.VMEM((CH, 32 * J, 128), F32),
            pltpu.VMEM((CH, 32 * J, 128), BF16),
            pltpu.VMEM((CH, 7, 4 * J, 128), BF16),
            pltpu.VMEM((CH, 4 * J, 128), BF16),
            pltpu.VMEM((CH, 4, J, 128), BF16),
            pltpu.VMEM((CH, J, 128), BF16),
            pltpu.VMEM((CH, 64 * J, 128), BF16),
            pltpu.VMEM((CH, 64 * J, 128), F32),
            pltpu.VMEM((3, 48, 128), F32),
            dma((CH + 6,)),
            dma((CH,)), dma((CH,)),
            dma((CH, 7)), dma((CH, 7)),
            dma((CH, 4)), dma((CH, 4)),
            dma((CH, 4)), dma((CH, 4)),
            dma((CH, 7)), dma((CH, 7)),
            dma((CH,)), dma((CH,)),
            dma, dma,
        ],
        compiler_params=pltpu.CompilerParams(
            collective_id=0, has_side_effects=True, vmem_limit_bytes=60 * 1024 * 1024
        ),
        cost_estimate=pl.CostEstimate(
            flops=4 * ROWS * TOK * D, bytes_accessed=6 * 1024 * 1024, transcendentals=0
        ),
    )(
        hidden[0].T,
        owner_order.reshape(1, ROWS),
        step_count,
        out_grad[0],
        weights_old,
        master.reshape(48, 128),
        first_moment.reshape(48, 128),
        second_moment.reshape(48, 128),
    )
    nm, nf, ns, ck, wn, hg = pl.pallas_call(
        write_out,
        out_shape=[jax.ShapeDtypeStruct(x.shape, x.dtype) for x in (nm, nf, ns, ck, wn, hg)],
        in_specs=[vmem] * 6,
        out_specs=[hbm] * 6,
        scratch_shapes=[dma((6,))],
        compiler_params=pltpu.CompilerParams(vmem_limit_bytes=2 * 1024 * 1024),
    )(nm, nf, ns, ck, wn, hg)
    return (
        nm.reshape(1, D), nf.reshape(1, D), ns.reshape(1, D),
        ck.reshape(3, 1, D), wn, hg.T[None],
    )


def solution(mesh):
    placed = (
        P("section", "replica", None),
        P("section", "replica", None),
        P("section", None),
        P(("section", "replica"), None),
        P(("section", "replica"), None),
        P(("section", "replica"), None),
        P(),
        P(),
    )
    return jax.shard_map(
        per_device,
        mesh=mesh,
        in_specs=placed,
        out_specs=(
            P(("section", "replica"), None),
            P(("section", "replica"), None),
            P(("section", "replica"), None),
            P(None, ("section", "replica"), None),
            P("section", None),
            P("section", "replica", None),
        ),
        check_vma=False,
    )
```

```python
import jax
import jax.numpy as jnp
from jax import lax
from jax.experimental import pallas as pl
from jax.experimental.pallas import tpu as pltpu
from jax.sharding import PartitionSpec as P

MESH = pl.DeviceIdType.MESH
F32 = jnp.float32
BF16 = jnp.bfloat16

D = 6144
ROWS = 64
TOK = 256
CH = 3
W = D // CH
J = W // 128
FAR = (6, -6, 2, -2)
FLIPS = [(i, f) for i in (3, 2, 1, 0) for f in (1, 0) if (i, f) != (0, 0)]


def rep_of(p):
    c, xh, zl, zh = p // 32, (p // 16) % 2, (p // 4) % 4, p % 4
    return (zh * 4 + zl) * 4 + xh * 2 + c


def kernel(
    hid_hbm, own_hbm, step_ref, og_hbm, w_hbm, m_hbm, f_hbm, s_hbm,
    nm_ref, nf_ref, ns_ref, ck_ref, wn_ref, hg_ref,
    hid_ref, own_ref, m_ref, f_ref, s_ref, og, w, part, core_in, full, t1, in1, t2, in2, fresh, ag, wide, moved,
    ld_sem, core_s, core_r, s1, r1, s2, r2, sa, ra, sb, rb, sc, rc, sk, rk,
):
    r = lax.axis_index("replica")
    z, xh, c = r // 4, (r // 2) % 2, r % 2
    a, zl = z // 4, z % 4
    g = xh * 4 + (z + 2) % 4

    def rep(z_, x_, c_):
        return ((z_ + 32) % 16) * 4 + x_ * 2 + c_

    offs = [0, 1, -1, 2 - 4 * c]
    sib = rep(z, xh, 1 - c)
    nxt, prv = (r + 1) % 64, (r + 63) % 64
    near_to = [(rep(z + offs[i], (xh + f) % 2, c)) for i, f in FLIPS]
    near_from = [(rep(z - offs[i], (xh + f) % 2, c)) for i, f in FLIPS]
    far = [rep(z + d, xh, c) for d in FAR]

    def remote(src, dst, ssem, rsem, to):
        return pltpu.make_async_remote_copy(
            src_ref=src, dst_ref=dst, send_sem=ssem, recv_sem=rsem,
            device_id={"replica": to}, device_id_type=MESH,
        )

    loads = [
        pltpu.make_async_copy(own_hbm, own_ref, ld_sem.at[CH + 1]),
        pltpu.make_async_copy(hid_hbm, hid_ref, ld_sem.at[CH + 2]),
    ]
    for ch in range(CH):
        cols = pl.ds(ch * W, W)
        loads.append(pltpu.make_async_copy(og_hbm.at[:, cols], og.at[:, cols], ld_sem.at[ch]))
    loads += [
        pltpu.make_async_copy(w_hbm, w, ld_sem.at[CH]),
        pltpu.make_async_copy(m_hbm, m_ref, ld_sem.at[CH + 3]),
        pltpu.make_async_copy(f_hbm, f_ref, ld_sem.at[CH + 4]),
        pltpu.make_async_copy(s_hbm, s_ref, ld_sem.at[CH + 5]),
    ]
    for x in loads:
        x.start()

    barrier = pltpu.get_barrier_semaphore()
    for to in [sib, prv] + near_from + far:
        pl.semaphore_signal(barrier, inc=1, device_id={"replica": to}, device_id_type=MESH)

    loads[0].wait()
    loads[1].wait()
    k_i = lax.broadcasted_iota(jnp.int32, (ROWS, ROWS), 0)
    p_i = lax.broadcasted_iota(jnp.int32, (ROWS, ROWS), 1)
    owns = jnp.where(own_ref[...] == k_i, 1.0, 0.0).astype(BF16)
    places = jnp.where(k_i == rep_of(p_i), 1.0, 0.0).astype(BF16)
    at = jnp.dot(owns, places, preferred_element_type=F32).astype(BF16)
    hid = lax.dot_general(
        at, hid_ref[...], (((0,), (0,)), ((), ())), preferred_element_type=F32
    ).astype(BF16)

    sends = []

    def start(copy):
        copy.start()
        sends.append(copy)
        return copy

    mine = pl.ds(pl.multiple_of(c * 32, 32), 32)
    theirs = pl.ds(pl.multiple_of((1 - c) * 32, 32), 32)
    core = []
    for ch in range(CH):
        loads[2 + ch].wait()
        for n in range(W // 512):
            at_col = ch * W + n * 512
            part[ch, :, n * 512 : (n + 1) * 512] = jnp.dot(
                hid, og[:, at_col : at_col + 512], preferred_element_type=F32
            )
        if ch == 0:
            pl.semaphore_wait(barrier, 13)
        core.append(
            start(remote(part.at[ch, theirs], core_in.at[ch], core_s.at[ch], core_r.at[ch], sib))
        )

    near = []
    for ch in range(CH):
        core[ch].wait_recv()
        for j in range(J):
            lanes = pl.ds(j * 128, 128)
            full[ch, pl.ds(j, 32, stride=J), :] = part[ch, mine, lanes] + core_in[ch, :, lanes]
        t1[ch] = full[ch].astype(BF16)
        row = []
        for k, (i, f) in enumerate(FLIPS):
            there = ((xh + f) % 2) * 4 + (z + offs[i] + 18) % 4
            src = t1.at[ch, pl.ds(pl.multiple_of(there * 4 * J, 64), 4 * J)]
            row.append(start(remote(src, in1.at[ch, k], s1.at[ch, k], r1.at[ch, k], near_to[k])))
        near.append(row)

    loads[2 + CH].wait()

    def back_step(n, total):
        cols = pl.ds(pl.multiple_of(n * 512, 512), 512)
        return total + lax.dot_general(
            w[:, cols], og[:, cols], (((1,), (1,)), ((), ())), preferred_element_type=F32
        )

    back = lax.fori_loop(0, D // 512, back_step, jnp.zeros((ROWS, TOK), F32))
    hg_ref[...] = (back * D ** (-0.5)).astype(BF16)

    group = pl.ds(pl.multiple_of(g * 4 * J, 64), 4 * J)
    far_c = []
    for ch in range(CH):
        total = full[ch, group, :]
        for k in range(7):
            near[ch][k].wait_recv()
            total = total + in1[ch, k].astype(F32)
        t2[ch] = total.astype(BF16)
        row = []
        for d in range(4):
            block = ((z + FAR[d] + 16) % 16) // 4
            src = t2.at[ch, pl.ds(pl.multiple_of(block * J, J), J)]
            row.append(start(remote(src, in2.at[ch, d], s2.at[ch, d], r2.at[ch, d], far[d])))
        far_c.append(row)

    steps = jnp.full((J, 128), step_ref[0], jnp.int32)
    pow1 = jnp.full((J, 128), 1.0, F32)
    pow2 = pow1
    for n in range(1, 9):
        pow1 = pow1 * jnp.where(steps >= n, 0.9, 1.0).astype(F32)
        pow2 = pow2 * jnp.where(steps >= n, 0.95, 1.0).astype(F32)
    fix1, fix2 = 1.0 - pow1, 1.0 - pow2

    own_rows = pl.ds(pl.multiple_of((c * 32 + xh * 16 + zl * 4 + a) * J, J), J)
    for x in loads[3 + CH :]:
        x.wait()
    first_c = []
    for ch in range(CH):
        for d in range(4):
            far_c[ch][d].wait_recv()
        grads = in2[ch, 0].astype(F32) + in2[ch, 1].astype(F32)
        grads = grads + in2[ch, 2].astype(F32) + in2[ch, 3].astype(F32)
        grads = grads * (1.0 / TOK)
        at_rows = pl.ds(ch * J, J)
        master = m_ref[at_rows, :]
        new_f = 0.9 * f_ref[at_rows, :] + 0.1 * grads
        new_s = 0.95 * s_ref[at_rows, :] + 0.05 * grads * grads
        update = new_f / fix1 / (jnp.sqrt(new_s / fix2) + 1e-08)
        new_m = master - 0.05 * (update + 0.1 * master)
        fresh[ch] = new_m.astype(BF16)
        row = []
        for d in range(4):
            there = ag.at[ch, own_rows]
            row.append(start(remote(fresh.at[ch], there, sa.at[ch, d], ra.at[ch, d], far[d])))
        first_c.append(row)
        nm_ref[at_rows, :] = new_m
        nf_ref[at_rows, :] = new_f
        ns_ref[at_rows, :] = new_s
        moved[0, at_rows, :] = new_m
        moved[1, at_rows, :] = new_f
        moved[2, at_rows, :] = new_s

    ck = start(remote(moved, ck_ref, sk, rk, nxt))
    mine_g = pl.ds(pl.multiple_of((c * 8 + g) * 4 * J, 64), 4 * J)
    second_c = []
    for ch in range(CH):
        for d in range(4):
            first_c[ch][d].wait_recv()
        row = []
        for k in range(7):
            here = ag.at[ch, mine_g]
            row.append(start(remote(here, here, sb.at[ch, k], rb.at[ch, k], near_to[k])))
        second_c.append(row)

    half = pl.ds(pl.multiple_of(c * 32 * J, 512), 32 * J)
    third_c = []
    for ch in range(CH):
        for k in range(7):
            second_c[ch][k].wait_recv()
        here = ag.at[ch, half]
        third_c.append(start(remote(here, here, sc.at[ch], rc.at[ch], sib)))
    other = pl.ds(pl.multiple_of((1 - c) * 32 * J, 512), 32 * J)
    for ch in range(CH):
        wide[ch, half, :] = ag[ch, half, :].astype(F32)
    for ch in range(CH):
        third_c[ch].wait_recv()
        wide[ch, other, :] = ag[ch, other, :].astype(F32)
        for n in range(J // 4):
            rows = [
                wide[ch, pl.ds(4 * n + q, ROWS, stride=J), :].astype(BF16) for q in range(4)
            ]
            wn_ref[:, pl.ds(ch * W + n * 512, 512)] = jnp.dot(
                at, jnp.concatenate(rows, axis=1), preferred_element_type=F32
            ).astype(BF16)
    ck.wait_recv()
    for copy in sends:
        copy.wait_send()


def write_out(*refs):
    srcs, dsts, sems = refs[:6], refs[6:12], refs[12]
    copies = [pltpu.make_async_copy(a, b, sems.at[i]) for i, (a, b) in enumerate(zip(srcs, dsts))]
    for x in copies:
        x.start()
    for x in copies:
        x.wait()


def per_device(
    hidden, out_grad, weights_old, master, first_moment, second_moment, owner_order, step_count
):
    vmem = pl.BlockSpec(memory_space=pltpu.VMEM)
    hbm = pl.BlockSpec(memory_space=pltpu.HBM)
    own = pltpu.VMEM((48, 128), F32)
    dma = pltpu.SemaphoreType.DMA
    nm, nf, ns, ck, wn, hg = pl.pallas_call(
        kernel,
        out_shape=(
            own, own, own,
            pltpu.VMEM((3, 48, 128), F32),
            pltpu.VMEM((ROWS, D), BF16),
            pltpu.VMEM((ROWS, TOK), BF16),
        ),
        in_specs=[
            hbm, hbm, pl.BlockSpec(memory_space=pltpu.SMEM), hbm, hbm, hbm, hbm, hbm,
        ],
        out_specs=(vmem,) * 6,
        scratch_shapes=[
            pltpu.VMEM((ROWS, TOK), BF16),
            pltpu.VMEM((1, ROWS), jnp.int32),
            pltpu.VMEM((48, 128), F32),
            pltpu.VMEM((48, 128), F32),
            pltpu.VMEM((48, 128), F32),
            pltpu.VMEM((TOK, D), BF16),
            pltpu.VMEM((ROWS, D), BF16),
            pltpu.VMEM((CH, ROWS, W), F32),
            pltpu.VMEM((CH, 32, W), F32),
            pltpu.VMEM((CH, 32 * J, 128), F32),
            pltpu.VMEM((CH, 32 * J, 128), BF16),
            pltpu.VMEM((CH, 7, 4 * J, 128), BF16),
            pltpu.VMEM((CH, 4 * J, 128), BF16),
            pltpu.VMEM((CH, 4, J, 128), BF16),
            pltpu.VMEM((CH, J, 128), BF16),
            pltpu.VMEM((CH, 64 * J, 128), BF16),
            pltpu.VMEM((CH, 64 * J, 128), F32),
            pltpu.VMEM((3, 48, 128), F32),
            dma((CH + 6,)),
            dma((CH,)), dma((CH,)),
            dma((CH, 7)), dma((CH, 7)),
            dma((CH, 4)), dma((CH, 4)),
            dma((CH, 4)), dma((CH, 4)),
            dma((CH, 7)), dma((CH, 7)),
            dma((CH,)), dma((CH,)),
            dma, dma,
        ],
        compiler_params=pltpu.CompilerParams(
            collective_id=0, has_side_effects=True, vmem_limit_bytes=60 * 1024 * 1024
        ),
        cost_estimate=pl.CostEstimate(
            flops=4 * ROWS * TOK * D, bytes_accessed=6 * 1024 * 1024, transcendentals=0
        ),
    )(
        hidden[0].T,
        owner_order.reshape(1, ROWS),
        step_count,
        out_grad[0],
        weights_old,
        master.reshape(48, 128),
        first_moment.reshape(48, 128),
        second_moment.reshape(48, 128),
    )
    nm, nf, ns, ck, wn, hg = pl.pallas_call(
        write_out,
        out_shape=[jax.ShapeDtypeStruct(x.shape, x.dtype) for x in (nm, nf, ns, ck, wn, hg)],
        in_specs=[vmem] * 6,
        out_specs=[hbm] * 6,
        scratch_shapes=[dma((6,))],
        compiler_params=pltpu.CompilerParams(vmem_limit_bytes=2 * 1024 * 1024),
    )(nm, nf, ns, ck, wn, hg)
    return (
        nm.reshape(1, D), nf.reshape(1, D), ns.reshape(1, D),
        ck.reshape(3, 1, D), wn, hg.T[None],
    )


def solution(mesh):
    placed = (
        P("section", "replica", None),
        P("section", "replica", None),
        P("section", None),
        P(("section", "replica"), None),
        P(("section", "replica"), None),
        P(("section", "replica"), None),
        P(),
        P(),
    )
    return jax.shard_map(
        per_device,
        mesh=mesh,
        in_specs=placed,
        out_specs=(
            P(("section", "replica"), None),
            P(("section", "replica"), None),
            P(("section", "replica"), None),
            P(None, ("section", "replica"), None),
            P("section", None),
            P("section", "replica", None),
        ),
        check_vma=False,
    )
```

```python
import jax
import jax.numpy as jnp
from jax import lax
from jax.experimental import pallas as pl
from jax.experimental.pallas import tpu as pltpu
from jax.sharding import PartitionSpec as P

MESH = pl.DeviceIdType.MESH
F32 = jnp.float32
BF16 = jnp.bfloat16

D = 6144
ROWS = 64
TOK = 256
CH = 3
W = D // CH
J = W // 128
FAR = (6, -6, 2, -2)
FLIPS = [(i, f) for i in (3, 2, 1, 0) for f in (1, 0) if (i, f) != (0, 0)]


def rep_of(p):
    c, xh, zl, zh = p // 32, (p // 16) % 2, (p // 4) % 4, p % 4
    return (zh * 4 + zl) * 4 + xh * 2 + c


def kernel(
    hid_hbm, own_hbm, step_ref, og_hbm, w_hbm, m_hbm, f_hbm, s_hbm,
    nm_ref, nf_ref, ns_ref, ck_ref, wn_ref, hg_ref,
    hid_ref, own_ref, m_ref, f_ref, s_ref, og, w, part, core_in, full, t1, in1, t2, in2, fresh, ag, wide, moved,
    ld_sem, core_s, core_r, s1, r1, s2, r2, sa, ra, sb, rb, sc, rc, sk, rk,
):
    r = lax.axis_index("replica")
    z, xh, c = r // 4, (r // 2) % 2, r % 2
    a, zl = z // 4, z % 4
    g = xh * 4 + (z + 2) % 4

    def rep(z_, x_, c_):
        return ((z_ + 32) % 16) * 4 + x_ * 2 + c_

    offs = [0, 1, -1, 2 - 4 * c]
    sib = rep(z, xh, 1 - c)
    nxt, prv = (r + 1) % 64, (r + 63) % 64
    near_to = [(rep(z + offs[i], (xh + f) % 2, c)) for i, f in FLIPS]
    near_from = [(rep(z - offs[i], (xh + f) % 2, c)) for i, f in FLIPS]
    far = [rep(z + d, xh, c) for d in FAR]

    def remote(src, dst, ssem, rsem, to):
        return pltpu.make_async_remote_copy(
            src_ref=src, dst_ref=dst, send_sem=ssem, recv_sem=rsem,
            device_id={"replica": to}, device_id_type=MESH,
        )

    loads = [
        pltpu.make_async_copy(own_hbm, own_ref, ld_sem.at[CH + 1]),
        pltpu.make_async_copy(hid_hbm, hid_ref, ld_sem.at[CH + 2]),
    ]
    for ch in range(CH):
        cols = pl.ds(ch * W, W)
        loads.append(pltpu.make_async_copy(og_hbm.at[:, cols], og.at[:, cols], ld_sem.at[ch]))
    loads += [
        pltpu.make_async_copy(w_hbm, w, ld_sem.at[CH]),
        pltpu.make_async_copy(m_hbm, m_ref, ld_sem.at[CH + 3]),
        pltpu.make_async_copy(f_hbm, f_ref, ld_sem.at[CH + 4]),
        pltpu.make_async_copy(s_hbm, s_ref, ld_sem.at[CH + 5]),
    ]
    for x in loads:
        x.start()

    barrier = pltpu.get_barrier_semaphore()
    for to in [sib, prv] + near_from + far:
        pl.semaphore_signal(barrier, inc=1, device_id={"replica": to}, device_id_type=MESH)

    loads[0].wait()
    loads[1].wait()
    k_i = lax.broadcasted_iota(jnp.int32, (ROWS, ROWS), 0)
    p_i = lax.broadcasted_iota(jnp.int32, (ROWS, ROWS), 1)
    owns = jnp.where(own_ref[...] == k_i, 1.0, 0.0).astype(BF16)
    places = jnp.where(k_i == rep_of(p_i), 1.0, 0.0).astype(BF16)
    at = jnp.dot(owns, places, preferred_element_type=F32).astype(BF16)
    hid = lax.dot_general(
        at, hid_ref[...], (((0,), (0,)), ((), ())), preferred_element_type=F32
    ).astype(BF16)

    sends = []
    gone = []

    def start(copy):
        copy.start()
        sends.append(copy)
        return copy

    mine = pl.ds(pl.multiple_of(c * 32, 32), 32)
    theirs = pl.ds(pl.multiple_of((1 - c) * 32, 32), 32)
    core = []
    for ch in range(CH):
        loads[2 + ch].wait()
        for n in range(W // 512):
            at_col = ch * W + n * 512
            part[ch, :, n * 512 : (n + 1) * 512] = jnp.dot(
                hid, og[:, at_col : at_col + 512], preferred_element_type=F32
            )
        if ch == 0:
            pl.semaphore_wait(barrier, 13)
        core.append(
            start(remote(part.at[ch, theirs], core_in.at[ch], core_s.at[ch], core_r.at[ch], sib))
        )

    near = []
    for ch in range(CH):
        core[ch].wait_recv()
        for j in range(J):
            lanes = pl.ds(j * 128, 128)
            full[ch, pl.ds(j, 32, stride=J), :] = part[ch, mine, lanes] + core_in[ch, :, lanes]
        t1[ch] = full[ch].astype(BF16)
        row = []
        for k, (i, f) in enumerate(FLIPS):
            there = ((xh + f) % 2) * 4 + (z + offs[i] + 18) % 4
            src = t1.at[ch, pl.ds(pl.multiple_of(there * 4 * J, 64), 4 * J)]
            row.append(start(remote(src, in1.at[ch, k], s1.at[ch, k], r1.at[ch, k], near_to[k])))
        near.append(row)

    loads[2 + CH].wait()

    def back_step(n, total):
        cols = pl.ds(pl.multiple_of(n * 512, 512), 512)
        return total + lax.dot_general(
            w[:, cols], og[:, cols], (((1,), (1,)), ((), ())), preferred_element_type=F32
        )

    back = lax.fori_loop(0, D // 512, back_step, jnp.zeros((ROWS, TOK), F32))
    hg_ref[...] = (back * D ** (-0.5)).astype(BF16)

    group = pl.ds(pl.multiple_of(g * 4 * J, 64), 4 * J)
    far_c = []
    for ch in range(CH):
        total = full[ch, group, :]
        for k in range(7):
            near[ch][k].wait_recv()
            total = total + in1[ch, k].astype(F32)
        t2[ch] = total.astype(BF16)
        row = []
        for d in range(4):
            block = ((z + FAR[d] + 16) % 16) // 4
            src = t2.at[ch, pl.ds(pl.multiple_of(block * J, J), J)]
            row.append(start(remote(src, in2.at[ch, d], s2.at[ch, d], r2.at[ch, d], far[d])))
        far_c.append(row)

    steps = jnp.full((J, 128), step_ref[0], jnp.int32)
    pow1 = jnp.full((J, 128), 1.0, F32)
    pow2 = pow1
    for n in range(1, 9):
        pow1 = pow1 * jnp.where(steps >= n, 0.9, 1.0).astype(F32)
        pow2 = pow2 * jnp.where(steps >= n, 0.95, 1.0).astype(F32)
    fix1, fix2 = 1.0 - pow1, 1.0 - pow2

    own_rows = pl.ds(pl.multiple_of((c * 32 + xh * 16 + zl * 4 + a) * J, J), J)
    for x in loads[3 + CH :]:
        x.wait()
    gone += sends
    sends.clear()
    first_c = []
    for ch in range(CH):
        for d in range(4):
            far_c[ch][d].wait_recv()
        grads = in2[ch, 0].astype(F32) + in2[ch, 1].astype(F32)
        grads = grads + in2[ch, 2].astype(F32) + in2[ch, 3].astype(F32)
        grads = grads * (1.0 / TOK)
        at_rows = pl.ds(ch * J, J)
        master = m_ref[at_rows, :]
        new_f = 0.9 * f_ref[at_rows, :] + 0.1 * grads
        new_s = 0.95 * s_ref[at_rows, :] + 0.05 * grads * grads
        update = new_f / fix1 / (jnp.sqrt(new_s / fix2) + 1e-08)
        new_m = master - 0.05 * (update + 0.1 * master)
        fresh[ch] = new_m.astype(BF16)
        row = []
        for d in range(4):
            there = ag.at[ch, own_rows]
            row.append(start(remote(fresh.at[ch], there, sa.at[ch, d], ra.at[ch, d], far[d])))
        first_c.append(row)
        nm_ref[at_rows, :] = new_m
        nf_ref[at_rows, :] = new_f
        ns_ref[at_rows, :] = new_s
        moved[0, at_rows, :] = new_m
        moved[1, at_rows, :] = new_f
        moved[2, at_rows, :] = new_s

    ck = start(remote(moved, ck_ref, sk, rk, nxt))
    for copy in gone:
        copy.wait_send()
    mine_g = pl.ds(pl.multiple_of((c * 8 + g) * 4 * J, 64), 4 * J)
    second_c = []
    for ch in range(CH):
        for d in range(4):
            first_c[ch][d].wait_recv()
        row = []
        for k in range(7):
            here = ag.at[ch, mine_g]
            row.append(start(remote(here, here, sb.at[ch, k], rb.at[ch, k], near_to[k])))
        second_c.append(row)

    half = pl.ds(pl.multiple_of(c * 32 * J, 512), 32 * J)
    third_c = []
    for ch in range(CH):
        for k in range(7):
            second_c[ch][k].wait_recv()
        here = ag.at[ch, half]
        third_c.append(start(remote(here, here, sc.at[ch], rc.at[ch], sib)))
    for copy in sends[:-CH]:
        copy.wait_send()
    other = pl.ds(pl.multiple_of((1 - c) * 32 * J, 512), 32 * J)
    for ch in range(CH):
        wide[ch, half, :] = ag[ch, half, :].astype(F32)
    for ch in range(CH):
        third_c[ch].wait_recv()
        wide[ch, other, :] = ag[ch, other, :].astype(F32)
        for n in range(J // 4):
            rows = [
                wide[ch, pl.ds(4 * n + q, ROWS, stride=J), :].astype(BF16) for q in range(4)
            ]
            wn_ref[:, pl.ds(ch * W + n * 512, 512)] = jnp.dot(
                at, jnp.concatenate(rows, axis=1), preferred_element_type=F32
            ).astype(BF16)
    ck.wait_recv()
    for copy in sends[-CH:]:
        copy.wait_send()


def write_out(*refs):
    srcs, dsts, sems = refs[:6], refs[6:12], refs[12]
    copies = [pltpu.make_async_copy(a, b, sems.at[i]) for i, (a, b) in enumerate(zip(srcs, dsts))]
    for x in copies:
        x.start()
    for x in copies:
        x.wait()


def per_device(
    hidden, out_grad, weights_old, master, first_moment, second_moment, owner_order, step_count
):
    vmem = pl.BlockSpec(memory_space=pltpu.VMEM)
    hbm = pl.BlockSpec(memory_space=pltpu.HBM)
    own = pltpu.VMEM((48, 128), F32)
    dma = pltpu.SemaphoreType.DMA
    nm, nf, ns, ck, wn, hg = pl.pallas_call(
        kernel,
        out_shape=(
            own, own, own,
            pltpu.VMEM((3, 48, 128), F32),
            pltpu.VMEM((ROWS, D), BF16),
            pltpu.VMEM((ROWS, TOK), BF16),
        ),
        in_specs=[
            hbm, hbm, pl.BlockSpec(memory_space=pltpu.SMEM), hbm, hbm, hbm, hbm, hbm,
        ],
        out_specs=(vmem,) * 6,
        scratch_shapes=[
            pltpu.VMEM((ROWS, TOK), BF16),
            pltpu.VMEM((1, ROWS), jnp.int32),
            pltpu.VMEM((48, 128), F32),
            pltpu.VMEM((48, 128), F32),
            pltpu.VMEM((48, 128), F32),
            pltpu.VMEM((TOK, D), BF16),
            pltpu.VMEM((ROWS, D), BF16),
            pltpu.VMEM((CH, ROWS, W), F32),
            pltpu.VMEM((CH, 32, W), F32),
            pltpu.VMEM((CH, 32 * J, 128), F32),
            pltpu.VMEM((CH, 32 * J, 128), BF16),
            pltpu.VMEM((CH, 7, 4 * J, 128), BF16),
            pltpu.VMEM((CH, 4 * J, 128), BF16),
            pltpu.VMEM((CH, 4, J, 128), BF16),
            pltpu.VMEM((CH, J, 128), BF16),
            pltpu.VMEM((CH, 64 * J, 128), BF16),
            pltpu.VMEM((CH, 64 * J, 128), F32),
            pltpu.VMEM((3, 48, 128), F32),
            dma((CH + 6,)),
            dma((CH,)), dma((CH,)),
            dma((CH, 7)), dma((CH, 7)),
            dma((CH, 4)), dma((CH, 4)),
            dma((CH, 4)), dma((CH, 4)),
            dma((CH, 7)), dma((CH, 7)),
            dma((CH,)), dma((CH,)),
            dma, dma,
        ],
        compiler_params=pltpu.CompilerParams(
            collective_id=0, has_side_effects=True, vmem_limit_bytes=60 * 1024 * 1024
        ),
        cost_estimate=pl.CostEstimate(
            flops=4 * ROWS * TOK * D, bytes_accessed=6 * 1024 * 1024, transcendentals=0
        ),
    )(
        hidden[0].T,
        owner_order.reshape(1, ROWS),
        step_count,
        out_grad[0],
        weights_old,
        master.reshape(48, 128),
        first_moment.reshape(48, 128),
        second_moment.reshape(48, 128),
    )
    nm, nf, ns, ck, wn, hg = pl.pallas_call(
        write_out,
        out_shape=[jax.ShapeDtypeStruct(x.shape, x.dtype) for x in (nm, nf, ns, ck, wn, hg)],
        in_specs=[vmem] * 6,
        out_specs=[hbm] * 6,
        scratch_shapes=[dma((6,))],
        compiler_params=pltpu.CompilerParams(vmem_limit_bytes=2 * 1024 * 1024),
    )(nm, nf, ns, ck, wn, hg)
    return (
        nm.reshape(1, D), nf.reshape(1, D), ns.reshape(1, D),
        ck.reshape(3, 1, D), wn, hg.T[None],
    )


def solution(mesh):
    placed = (
        P("section", "replica", None),
        P("section", "replica", None),
        P("section", None),
        P(("section", "replica"), None),
        P(("section", "replica"), None),
        P(("section", "replica"), None),
        P(),
        P(),
    )
    return jax.shard_map(
        per_device,
        mesh=mesh,
        in_specs=placed,
        out_specs=(
            P(("section", "replica"), None),
            P(("section", "replica"), None),
            P(("section", "replica"), None),
            P(None, ("section", "replica"), None),
            P("section", None),
            P("section", "replica", None),
        ),
        check_vma=False,
    )
```
